768 devices in a mesh: dp: 96 (over y_lo, z, core), pack: 8 (over x, y_hi).
Axes of the slice: x: 4, y: 8 (y_hi: 2, y_lo: 4; y = y_hi * 4 + y_lo), z: 12, core: 2. Of those that a mesh axis runs over, the one named last changes fastest.
Arguments:
- images: bfloat16 [1536, 1152], P(('dp', 'pack')), may hold values from -6 to 6
- captions: bfloat16 [3072, 1152], P(('dp', 'pack')), may hold values from -6 to 6
- caption_owner: int32 [3072], P(('dp', 'pack')), may hold values from 0 to 15, as said below
- caption_count: int32 [768], P(('dp', 'pack')), may hold values from 0 to 4, as said below
- log_scale: float32 [1], replicated, may hold values from 1.6 to 2.6
- bias: float32 [1], replicated, may hold values from -3 to 0
Outputs:
- row_loss: float32 [1536], P(('dp', 'pack'))
- grad_images: float32 [1536, 1152], P(('dp', 'pack'))
- grad_captions: float32 [3072, 1152], P(('dp', 'pack'))
The draws below stay inside these ranges and needn't reach their ends.
Inputs may be any that keep to these rules, and one draw needn't show every extreme that they name: `caption_owner`: within each pair block, the filled slots of its 8 devices name every one of its 16 pairs exactly once; values in empty slots are arbitrary. `caption_count`: the counts of one pair block's devices sum to 16.
All inputs are finite; a program needn't handle non-finite values.
Results may differ from the reference program's by a relative error of at most 0.0043.
Values may be sent and summed in bfloat16 or wider, within the bound.
A program may use at most 32 MiB of HBM per device.

```python
import jax
import jax.numpy as jnp
from jax import lax

D = 1152
PAIR_DEV = 2
SLOTS = 4
PAIRS = 1536
N_DP = 96
N_PACK = 8


def packing_plan(key):
    group_rows = PAIR_DEV * N_PACK
    key_weight, key_big, key_perm, key_fill = jax.random.split(key, 4)
    biggest = jax.random.randint(key_big, (N_DP,), 0, N_PACK)
    device_ids = jnp.arange(N_PACK, dtype=jnp.int32)[None, :]
    is_big = device_ids == biggest[:, None]
    shares = jax.random.randint(key_weight, (N_DP, N_PACK), 2, 4)
    shares = jnp.where(is_big, 0, shares)
    remain = (N_PACK - 2) * PAIR_DEV
    counts = remain * shares // jnp.sum(shares, axis=1, keepdims=True)
    deficit = remain - jnp.sum(counts, axis=1, keepdims=True)
    ranked = device_ids - (device_ids > biggest[:, None]).astype(jnp.int32)
    counts = counts + jnp.where(jnp.logical_and(ranked < deficit, jnp.logical_not(is_big)), 1, 0)
    counts = jnp.where(is_big, 2 * PAIR_DEV, counts).astype(jnp.int32)
    offsets = jnp.cumsum(counts, axis=1) - counts
    perm_keys = jax.random.split(key_perm, N_DP)
    orders = jax.vmap(lambda one_key: jax.random.permutation(one_key, group_rows))(perm_keys).astype(jnp.int32)
    filler = jax.random.randint(key_fill, (N_DP, N_PACK, SLOTS), 0, group_rows)
    slot_ids = jnp.arange(SLOTS, dtype=jnp.int32)[None, None, :]
    places = offsets[:, :, None] + slot_ids
    filled = slot_ids < counts[:, :, None]
    places = jnp.clip(places, 0, group_rows - 1).reshape(N_DP, N_PACK * SLOTS)
    taken = jnp.take_along_axis(orders, places, axis=1).reshape(N_DP, N_PACK, SLOTS)
    owners = jnp.where(filled, taken, filler).astype(jnp.int32)
    return (owners.reshape(N_DP * N_PACK * SLOTS), counts.reshape(N_DP * N_PACK))


def draw_caption_owner(key, part):
    owners, counts = packing_plan(key)
    return owners


def draw_caption_count(key, part):
    owners, counts = packing_plan(key)
    return counts


def block_scale(stream_key, shape, pieces, smallest, top_value):
    loudness, own = 1.0, jax.random.fold_in(stream_key, 6)
    for axis_at, shards_of in pieces:
        steps = jnp.exp(jax.random.uniform(jax.random.fold_in(own, axis_at), (shards_of,), jnp.float32, smallest / len(pieces), top_value / len(pieces)))
        loudness = loudness * jnp.repeat(steps, shape[axis_at] // shards_of).reshape([-1 if axis == axis_at else 1 for axis in range(len(shape))])
    return loudness


def scatter_about(key, extent, width, bound, cuts=(), held_as=jnp.bfloat16):
    array = jax.random.normal(key, extent, jnp.float32) * width
    if len(cuts) > 0:
        array = block_scale(key, extent, cuts, -0.22, 0.18) * array
    return jnp.clip(array, min=-bound, max=bound).astype(held_as)


def setup_inputs(seed: int = 0) -> dict:
    streams_of = jax.random.split(jax.random.key(seed), 7)
    images = scatter_about(streams_of[0], (PAIRS, D), 1.0, 6.0, ((0, 768),))
    captions = scatter_about(streams_of[1], (N_DP * N_PACK * SLOTS, D), 1.0, 6.0, ((0, 768),))
    caption_owner = draw_caption_owner(jax.random.fold_in(streams_of[6], 71), 0)
    caption_count = draw_caption_count(jax.random.fold_in(streams_of[6], 71), 0)
    log_scale = jnp.clip(jax.random.uniform(streams_of[4], (1,), jnp.float32, 1.6, 2.6), 1.6, 2.6)
    bias = jnp.clip(jax.random.uniform(streams_of[5], (1,), jnp.float32, -3.0, 0.0), -3.0, 0.0)
    return {"images": images, "captions": captions, "caption_owner": caption_owner, "caption_count": caption_count, "log_scale": log_scale, "bias": bias}


eps = 1e-06

def normalize(block_rows):
    floats = block_rows.astype(jnp.float32)
    inverse = lax.rsqrt(lax.optimization_barrier(jnp.sum(floats * floats, axis=-1, keepdims=True)) + eps)
    return (floats * inverse, inverse)

def unnormalize(unit_rows, inverse, upstream):
    return inverse * (upstream - unit_rows * lax.optimization_barrier(jnp.sum(unit_rows * upstream, axis=-1, keepdims=True)))

def reference(images, captions, caption_owner, caption_count, log_scale, bias):
    group_rows = PAIR_DEV * N_PACK
    slot_ids = jnp.arange(N_DP * N_PACK * SLOTS, dtype=jnp.int32)
    device_ids = slot_ids // SLOTS
    filled = slot_ids % SLOTS < caption_count[device_ids]
    target = device_ids // N_PACK * group_rows + caption_owner
    target = jnp.where(filled, target, PAIRS).astype(jnp.int32)
    owned_texts = jax.ops.segment_sum(captions.astype(jnp.float32), target, num_segments=PAIRS + 1)[:PAIRS].astype(jnp.bfloat16)
    image_unit, image_inv = normalize(images)
    image16 = image_unit.astype(jnp.bfloat16)
    text_unit, text_inv = normalize(owned_texts)
    text16 = text_unit.astype(jnp.bfloat16)
    logit_scale = jnp.exp(log_scale[0])
    logit_shift = bias[0]
    columns = jnp.arange(PAIRS, dtype=jnp.int32)

    def block_step(running, block_index):
        block_rows = lax.dynamic_slice_in_dim(image16, block_index * group_rows, group_rows, 0)
        logits = logit_scale * jnp.dot(block_rows, text16.T, preferred_element_type=jnp.float32) + logit_shift
        row_ids = block_index * group_rows + jnp.arange(group_rows, dtype=jnp.int32)
        labels = jnp.where(row_ids[:, None] == columns[None, :], 1.0, -1.0).astype(jnp.float32)
        losses = lax.optimization_barrier(jnp.sum(jax.nn.softplus(-labels * logits), axis=1)) / PAIRS
        weights = (-labels * jax.nn.sigmoid(-labels * logits)).astype(jnp.bfloat16)
        grad_rows = logit_scale * jnp.dot(weights, text16, preferred_element_type=jnp.float32)
        text_term = lax.dot_general(weights, block_rows, (((0,), (0,)), ((), ())), preferred_element_type=jnp.float32)
        return (running + text_term, (losses, grad_rows))
    text_sum, (losses, grad_unit) = lax.scan(block_step, jnp.zeros((PAIRS, D), jnp.float32), jnp.arange(N_DP, dtype=jnp.int32))
    row_loss = losses.reshape(PAIRS)
    grad_images = unnormalize(image_unit, image_inv, grad_unit.reshape(PAIRS, D))
    grad_texts = unnormalize(text_unit, text_inv, logit_scale * text_sum)
    picked = grad_texts[jnp.minimum(target, PAIRS - 1)]
    grad_captions = jnp.where(filled[:, None], picked, 0.0).astype(jnp.float32)
    return (row_loss, grad_images, grad_captions)
```

```python
import functools

import jax
import jax.numpy as jnp
from jax import lax
from jax.experimental import pallas as pl
from jax.experimental.pallas import tpu as pltpu
from jax.sharding import PartitionSpec as P

MESH = pl.DeviceIdType.MESH
EPS = 1e-06
NX, Y_HI, Y_LO, NZ = 4, 2, 4, 12
PAIR, SLOT = 2, 4
EXTRA = 128


def normalize(rows):
    inverse = lax.rsqrt(jnp.sum(rows * rows, axis=-1, keepdims=True) + EPS)
    return rows * inverse, inverse


def unnormalize(unit, inverse, upstream):
    return inverse * (upstream - unit * jnp.sum(unit * upstream, axis=-1, keepdims=True))


def softplus(v):
    return jnp.maximum(v, 0.0) + jnp.log1p(jnp.exp(-jnp.abs(v)))


def split_sum(total):
    high = total.astype(jnp.bfloat16)
    low = (total - high.astype(jnp.float32)).astype(jnp.bfloat16)
    lane = lax.broadcasted_iota(jnp.int32, (total.shape[0], EXTRA), 1)
    return jnp.where(lane == 0, high.astype(jnp.float32), jnp.where(lane == 1, low.astype(jnp.float32), 0.0))


def kernel(
    all_pairs,
    images_ref, captions_ref, owner_ref, count_ref, scale_ref, bias_ref,
    loss_ref, gi_ref, gc_ref,
    y_in, z_in, x_all, texts,
    core_out, core_in, x_out, x_in, y_out, y_back, z_out, z_back,
    send, recv,
):
    D = images_ref.shape[1]
    ny = Y_HI * Y_LO
    rows_y = PAIR * ny
    dp = lax.axis_index("dp")
    pack = lax.axis_index("pack")
    core = lax.rem(dp, 2)
    z = lax.rem(dp // 2, NZ)
    y_lo = dp // (2 * NZ)
    x = pack // Y_HI
    y_hi = lax.rem(pack, Y_HI)
    y = y_hi * Y_LO + y_lo

    def device(xx, yy, zz, cc):
        return ((lax.rem(yy, Y_LO) * NZ + zz) * 2 + cc, xx * Y_HI + yy // Y_LO)

    def at_x(k):
        return device(lax.rem(x + k + NX, NX), y, z, core)

    def at_y(k):
        return device(x, lax.rem(y + k + ny, ny), z, core)

    def at_z(k):
        return device(x, y, lax.rem(z + k + NZ, NZ), core)

    sibling = device(x, y, z, 1 - core)

    barrier = pltpu.get_barrier_semaphore()
    partners = [sibling]
    partners += [at_x(k) for k in range(1, NX)]
    partners += [at_y(k) for k in range(1, ny)]
    partners += [at_z(k) for k in range(1, NZ)]
    for partner in partners:
        pl.semaphore_signal(barrier, inc=1, device_id=partner, device_id_type=MESH)

    image_unit, image_inv = normalize(images_ref[...].astype(jnp.float32))
    y_in[0] = image_unit.astype(jnp.bfloat16)
    slot_row = lax.broadcasted_iota(jnp.int32, (SLOT, 1), 0)
    filled = slot_row < count_ref[0]
    captions = jnp.where(filled, captions_ref[...].astype(jnp.float32), 0.0)
    text_unit, text_inv = normalize(captions)
    z_in[0] = text_unit.astype(jnp.bfloat16)

    pl.semaphore_wait(barrier, len(partners))

    def copy(src, dst, sem, to):
        pltpu.make_async_remote_copy(
            src_ref=src, dst_ref=dst, send_sem=send.at[sem], recv_sem=recv.at[sem],
            device_id=to, device_id_type=MESH,
        ).start()

    def arrived(ref, sem):
        pltpu.make_async_copy(ref, ref, recv.at[sem]).wait()

    def left(ref, sem):
        pltpu.make_async_copy(ref, ref, send.at[sem]).wait()

    for k in range(1, ny):
        copy(y_in.at[0], y_in.at[k], 0, at_y(k))
    for k in range(1, NZ):
        copy(z_in.at[0], z_in.at[k], 1, at_z(k))

    arrived(y_in.at[pl.ds(1, ny - 1)], 0)
    x_all[0, 0] = jnp.concatenate([y_in[k].astype(jnp.float32) for k in range(ny)], axis=0).astype(jnp.bfloat16)
    for k in range(1, NX):
        copy(x_all.at[0, 0], x_all.at[0, k], 2, at_x(k))
    copy(x_all.at[0, 0], x_all.at[1, 0], 3, sibling)

    arrived(z_in.at[pl.ds(1, NZ - 1)], 1)
    texts[...] = jnp.concatenate([z_in[k].astype(jnp.float32) for k in range(NZ)], axis=0).astype(jnp.bfloat16)

    arrived(x_all.at[0, pl.ds(1, NX - 1)], 2)
    copy(x_all.at[0, pl.ds(1, NX - 1)], x_all.at[1, pl.ds(1, NX - 1)], 4, sibling)

    rows = NX * rows_y
    own = lax.broadcasted_iota(jnp.int32, (2 * rows, NZ * SLOT), 0)
    column = lax.broadcasted_iota(jnp.int32, (2 * rows, NZ * SLOT), 1)
    from_x = lax.rem(x - lax.rem(own // rows_y, NX) + NX, NX)
    y_slot = lax.rem(own, rows_y) // PAIR
    from_y_hi = lax.rem(y_hi - y_slot // Y_LO + Y_HI, Y_HI)
    pair = (from_x * Y_HI + from_y_hi) * PAIR + lax.rem(own, PAIR)
    pair = jnp.where(jnp.logical_and(own < rows, lax.rem(y_slot, Y_LO) == 0), pair, -1)
    owner = jnp.full_like(column, -2)
    for s in range(SLOT):
        owner = jnp.where(jnp.logical_and(column == s, s < count_ref[0]), owner_ref[s], owner)
    sign = jnp.where(pair == owner, -1.0, 1.0)

    scale = jnp.exp(jnp.full((1, 1), scale_ref[0], jnp.float32))
    bias = jnp.full((1, 1), bias_ref[0], jnp.float32)

    arrived(x_all.at[1, 0], 3)
    arrived(x_all.at[1, pl.ds(1, NX - 1)], 4)

    image_rows = x_all[...].reshape(2 * rows, D)
    text_rows = texts[...]
    dots = lax.dot_general(image_rows, text_rows, (((1,), (1,)), ((), ())), preferred_element_type=jnp.float32)
    v = sign * (scale * dots + bias)
    small = jnp.exp(-jnp.abs(v))
    losses = jnp.sum(jnp.maximum(v, 0.0) + jnp.log1p(small), axis=1, keepdims=True)
    weights = (sign * jnp.where(v >= 0.0, 1.0, small) / (1.0 + small)).astype(jnp.bfloat16)

    core_out[:, :D] = (scale * jnp.dot(weights[rows:], text_rows, preferred_element_type=jnp.float32)).astype(jnp.bfloat16)
    core_out[:, D:] = split_sum(losses[rows:]).astype(jnp.bfloat16)
    copy(core_out, core_in, 5, sibling)

    text_grad = scale * lax.dot_general(weights, image_rows, (((0,), (0,)), ((), ())), preferred_element_type=jnp.float32)
    for k in range(1, NZ):
        z_out[k] = text_grad[k * SLOT:(k + 1) * SLOT].astype(jnp.bfloat16)
        copy(z_out.at[k], z_back.at[k], 6, at_z(-k))

    mine = scale * jnp.dot(weights[:rows], text_rows, preferred_element_type=jnp.float32)
    arrived(core_in, 5)
    mine = mine + core_in[:, :D].astype(jnp.float32)
    other = core_in[:, D:].astype(jnp.float32)
    loss = losses[:rows] + jnp.sum(other, axis=1, keepdims=True)
    for k in range(1, NX):
        part = slice(k * rows_y, (k + 1) * rows_y)
        x_out[k, :, :D] = mine[part].astype(jnp.bfloat16)
        x_out[k, :, D:] = split_sum(loss[part]).astype(jnp.bfloat16)
        copy(x_out.at[k], x_in.at[k], 7, at_x(-k))
    mine, loss = mine[:rows_y], loss[:rows_y]

    arrived(x_in.at[pl.ds(1, NX - 1)], 7)
    for k in range(1, NX):
        mine = mine + x_in[k, :, :D].astype(jnp.float32)
        loss = loss + jnp.sum(x_in[k, :, D:].astype(jnp.float32), axis=1, keepdims=True)
    pieces = split_sum(loss)
    for k in range(1, ny):
        part = slice(k * PAIR, (k + 1) * PAIR)
        y_out[k, :, :D] = mine[part].astype(jnp.bfloat16)
        y_out[k, :, D:] = pieces[part].astype(jnp.bfloat16)
        copy(y_out.at[k], y_back.at[k], 8, at_y(-k))
    mine, loss = mine[:PAIR], loss[:PAIR]

    text_mine = text_grad[:SLOT]
    arrived(z_back.at[pl.ds(1, NZ - 1)], 6)
    for k in range(1, NZ):
        text_mine = text_mine + z_back[k].astype(jnp.float32)
    gc_ref[...] = jnp.where(filled, unnormalize(text_unit, text_inv, text_mine), 0.0)

    arrived(y_back.at[pl.ds(1, ny - 1)], 8)
    for k in range(1, ny):
        mine = mine + y_back[k, :, :D].astype(jnp.float32)
        loss = loss + jnp.sum(y_back[k, :, D:].astype(jnp.float32), axis=1, keepdims=True)
    gi_ref[...] = unnormalize(image_unit, image_inv, mine)
    loss_ref[...] = jnp.broadcast_to(loss / all_pairs - softplus(bias), loss_ref.shape)

    left(y_in.at[pl.ds(1, ny - 1)], 0)
    left(z_in.at[pl.ds(1, NZ - 1)], 1)
    left(x_all.at[0, pl.ds(1, NX - 1)], 2)
    left(x_all.at[1, 0], 3)
    left(x_all.at[1, pl.ds(1, NX - 1)], 4)
    left(core_out, 5)
    left(z_out.at[pl.ds(1, NZ - 1)], 6)
    left(x_out.at[pl.ds(1, NX - 1)], 7)
    left(y_out.at[pl.ds(1, ny - 1)], 8)


def body(images, captions, caption_owner, caption_count, log_scale, bias):
    D = images.shape[1]
    W = D + EXTRA
    ny = Y_HI * Y_LO
    rows_y = PAIR * ny
    rows = NX * rows_y
    all_pairs = PAIR * 2 * NX * ny * NZ
    vmem = pl.BlockSpec(memory_space=pltpu.VMEM)
    smem = pl.BlockSpec(memory_space=pltpu.SMEM)
    half = jnp.bfloat16
    loss, gi, gc = pl.pallas_call(
        functools.partial(kernel, all_pairs),
        out_shape=(
            jax.ShapeDtypeStruct((PAIR, 128), jnp.float32),
            jax.ShapeDtypeStruct((PAIR, D), jnp.float32),
            jax.ShapeDtypeStruct((SLOT, D), jnp.float32),
        ),
        in_specs=[vmem, vmem, smem, smem, smem, smem],
        out_specs=(vmem, vmem, vmem),
        scratch_shapes=[
            pltpu.VMEM((ny, PAIR, D), half),
            pltpu.VMEM((NZ, SLOT, D), half),
            pltpu.VMEM((2, NX, rows_y, D), half),
            pltpu.VMEM((NZ * SLOT, D), half),
            pltpu.VMEM((rows, W), half),
            pltpu.VMEM((rows, W), half),
            pltpu.VMEM((NX, rows_y, W), half),
            pltpu.VMEM((NX, rows_y, W), half),
            pltpu.VMEM((ny, PAIR, W), half),
            pltpu.VMEM((ny, PAIR, W), half),
            pltpu.VMEM((NZ, SLOT, D), half),
            pltpu.VMEM((NZ, SLOT, D), half),
            pltpu.SemaphoreType.DMA((9,)),
            pltpu.SemaphoreType.DMA((9,)),
        ],
        compiler_params=pltpu.CompilerParams(
            collective_id=0, has_side_effects=True, vmem_limit_bytes=32 * 1024 * 1024
        ),
    )(images, captions, caption_owner, caption_count, log_scale, bias)
    return loss[:, 0], gi, gc


def solution(mesh):
    placed = (
        P(("dp", "pack"), None),
        P(("dp", "pack"), None),
        P(("dp", "pack")),
        P(("dp", "pack")),
        P(),
        P(),
    )
    return jax.shard_map(
        body,
        mesh=mesh,
        in_specs=placed,
        out_specs=(P(("dp", "pack")), P(("dp", "pack"), None), P(("dp", "pack"), None)),
        check_vma=False,
    )
```

```python
import functools

import jax
import jax.numpy as jnp
from jax import lax
from jax.experimental import pallas as pl
from jax.experimental.pallas import tpu as pltpu
from jax.sharding import PartitionSpec as P

MESH = pl.DeviceIdType.MESH
EPS = 1e-06
NX, Y_HI, Y_LO, NZ = 4, 2, 4, 12
PAIR, SLOT = 2, 4
EXTRA = 128


def normalize(rows):
    inverse = lax.rsqrt(jnp.sum(rows * rows, axis=-1, keepdims=True) + EPS)
    return rows * inverse, inverse


def unnormalize(unit, inverse, upstream):
    return inverse * (upstream - unit * jnp.sum(unit * upstream, axis=-1, keepdims=True))


def softplus(v):
    return jnp.maximum(v, 0.0) + jnp.log1p(jnp.exp(-jnp.abs(v)))


def split_sum(total):
    high = total.astype(jnp.bfloat16)
    low = (total - high.astype(jnp.float32)).astype(jnp.bfloat16)
    lane = lax.broadcasted_iota(jnp.int32, (total.shape[0], EXTRA), 1)
    return jnp.where(lane == 0, high.astype(jnp.float32), jnp.where(lane == 1, low.astype(jnp.float32), 0.0))


def kernel(
    all_pairs,
    images_hbm, captions_hbm, owner_hbm, count_ref, scale_ref, bias_ref,
    loss_ref, gi_ref, gc_ref,
    images_ref, captions_ref, owner_ref,
    xy_in, z_in, x_all, texts,
    core_out, core_in, xy_out, xy_back, z_out, z_back,
    load, send, recv,
):
    D = images_ref.shape[1]
    ny = Y_HI * Y_LO
    nxy = NX * ny
    rows = PAIR * nxy
    loads = [
        pltpu.make_async_copy(src, dst, load.at[i])
        for i, (src, dst) in enumerate((
            (images_hbm, images_ref), (captions_hbm, captions_ref), (owner_hbm, owner_ref),
        ))
    ]
    for one in loads:
        one.start()
    dp = lax.axis_index("dp")
    pack = lax.axis_index("pack")
    core = lax.rem(dp, 2)
    z = lax.rem(dp // 2, NZ)
    y_lo = dp // (2 * NZ)
    x = pack // Y_HI
    y_hi = lax.rem(pack, Y_HI)
    y = y_hi * Y_LO + y_lo

    def device(xx, yy, zz, cc):
        return ((lax.rem(yy, Y_LO) * NZ + zz) * 2 + cc, xx * Y_HI + yy // Y_LO)

    def at_xy(k, way):
        kx, ky = k % NX, k // NX
        return device(lax.rem(x + way * kx + NX, NX), lax.rem(y + way * ky + ny, ny), z, core)

    def at_z(k):
        return device(x, y, lax.rem(z + k + NZ, NZ), core)

    sibling = device(x, y, z, 1 - core)

    def hops(k, n):
        return min(k, n - k)

    far_xy = sorted(range(1, nxy), key=lambda k: -hops(k % NX, NX) - hops(k // NX, ny))
    far_z = sorted(range(1, NZ), key=lambda k: -hops(k, NZ))

    barrier = pltpu.get_barrier_semaphore()
    partners = [sibling]
    partners += [at_z(k) for k in far_z]
    partners += [at_xy(k, 1) for k in far_xy]
    for partner in partners:
        pl.semaphore_signal(barrier, inc=1, device_id=partner, device_id_type=MESH)

    loads[0].wait()
    image_unit, image_inv = normalize(images_ref[...].astype(jnp.float32))
    xy_in[0] = image_unit.astype(jnp.bfloat16)
    loads[1].wait()
    slot_row = lax.broadcasted_iota(jnp.int32, (SLOT, 1), 0)
    filled = slot_row < count_ref[0]
    captions = jnp.where(filled, captions_ref[...].astype(jnp.float32), 0.0)
    text_unit, text_inv = normalize(captions)
    z_in[0] = text_unit.astype(jnp.bfloat16)

    pl.semaphore_wait(barrier, len(partners))

    sent = []

    def copy(src, dst, sem, to):
        pltpu.make_async_remote_copy(
            src_ref=src, dst_ref=dst, send_sem=send.at[sem], recv_sem=recv.at[sem],
            device_id=to, device_id_type=MESH,
        ).start()

    def arrived(ref, sem):
        pltpu.make_async_copy(ref, ref, recv.at[sem]).wait()

    for k in far_z:
        copy(z_in.at[0], z_in.at[k], 1, at_z(k))
    sent.append((z_in.at[pl.ds(1, NZ - 1)], 1))
    for k in far_xy:
        copy(xy_in.at[0], xy_in.at[k], 0, at_xy(k, 1))
    sent.append((xy_in.at[pl.ds(1, nxy - 1)], 0))

    arrived(xy_in.at[pl.ds(1, nxy - 1)], 0)
    x_all[0] = jnp.concatenate([xy_in[k].astype(jnp.float32) for k in range(nxy)], axis=0).astype(jnp.bfloat16)
    copy(x_all.at[0], x_all.at[1], 3, sibling)
    sent.append((x_all.at[1], 3))

    arrived(z_in.at[pl.ds(1, NZ - 1)], 1)
    texts[...] = jnp.concatenate([z_in[k].astype(jnp.float32) for k in range(NZ)], axis=0).astype(jnp.bfloat16)

    loads[2].wait()
    own = lax.broadcasted_iota(jnp.int32, (2 * rows, NZ * SLOT), 0)
    column = lax.broadcasted_iota(jnp.int32, (2 * rows, NZ * SLOT), 1)
    slot = lax.rem(own, rows) // PAIR
    y_slot = slot // NX
    from_x = lax.rem(x - lax.rem(slot, NX) + NX, NX)
    from_y_hi = lax.rem(y_hi - y_slot // Y_LO + Y_HI, Y_HI)
    pair = (from_x * Y_HI + from_y_hi) * PAIR + lax.rem(own, PAIR)
    pair = jnp.where(jnp.logical_and(own < rows, lax.rem(y_slot, Y_LO) == 0), pair, -1)
    owner = jnp.full_like(column, -2)
    for s in range(SLOT):
        owner = jnp.where(jnp.logical_and(column == s, s < count_ref[0]), owner_ref[s], owner)
    sign = jnp.where(pair == owner, -1.0, 1.0)

    scale = jnp.exp(jnp.full((1, 1), scale_ref[0], jnp.float32))
    bias = jnp.full((1, 1), bias_ref[0], jnp.float32)

    arrived(x_all.at[1], 3)

    image_rows = x_all[...].reshape(2 * rows, D)
    text_rows = texts[...]
    dots = lax.dot_general(image_rows, text_rows, (((1,), (1,)), ((), ())), preferred_element_type=jnp.float32)
    v = sign * (scale * dots + bias)
    small = jnp.exp(-jnp.abs(v))
    losses = jnp.sum(jnp.maximum(v, 0.0) + jnp.log1p(small), axis=1, keepdims=True)
    weights = (sign * jnp.where(v >= 0.0, 1.0, small) / (1.0 + small)).astype(jnp.bfloat16)

    core_out[:, :D] = (scale * jnp.dot(weights[rows:], text_rows, preferred_element_type=jnp.float32)).astype(jnp.bfloat16)
    core_out[:, D:] = split_sum(losses[rows:]).astype(jnp.bfloat16)
    copy(core_out, core_in, 5, sibling)
    sent.append((core_out, 5))

    text_grad = scale * lax.dot_general(weights, image_rows, (((0,), (0,)), ((), ())), preferred_element_type=jnp.float32)
    for k in far_z:
        z_out[k] = text_grad[k * SLOT:(k + 1) * SLOT].astype(jnp.bfloat16)
        copy(z_out.at[k], z_back.at[k], 6, at_z(-k))
    sent.append((z_out.at[pl.ds(1, NZ - 1)], 6))

    mine = scale * jnp.dot(weights[:rows], text_rows, preferred_element_type=jnp.float32)
    arrived(core_in, 5)
    mine = mine + core_in[:, :D].astype(jnp.float32)
    other = core_in[:, D:].astype(jnp.float32)
    loss = losses[:rows] + jnp.sum(other, axis=1, keepdims=True)
    pieces = split_sum(loss)
    for k in far_xy:
        part = slice(k * PAIR, (k + 1) * PAIR)
        xy_out[k, :, :D] = mine[part].astype(jnp.bfloat16)
        xy_out[k, :, D:] = pieces[part].astype(jnp.bfloat16)
        copy(xy_out.at[k], xy_back.at[k], 7, at_xy(k, -1))
    sent.append((xy_out.at[pl.ds(1, nxy - 1)], 7))
    mine, loss = mine[:PAIR], loss[:PAIR]

    text_mine = text_grad[:SLOT]
    arrived(z_back.at[pl.ds(1, NZ - 1)], 6)
    for k in range(1, NZ):
        text_mine = text_mine + z_back[k].astype(jnp.float32)
    gc_ref[...] = jnp.where(filled, unnormalize(text_unit, text_inv, text_mine), 0.0)

    arrived(xy_back.at[pl.ds(1, nxy - 1)], 7)
    for k in range(1, nxy):
        mine = mine + xy_back[k, :, :D].astype(jnp.float32)
        loss = loss + jnp.sum(xy_back[k, :, D:].astype(jnp.float32), axis=1, keepdims=True)
    gi_ref[...] = unnormalize(image_unit, image_inv, mine)
    loss_ref[...] = (loss / all_pairs - softplus(bias))[:, 0]

    for ref, sem in sent:
        pltpu.make_async_copy(ref, ref, send.at[sem]).wait()


def hand_over(loss_in, gi_in, gc_in, loss_ref, gi_ref, gc_ref):
    loss_ref[...] = loss_in[...]
    gi_ref[...] = gi_in[...]
    gc_ref[...] = gc_in[...]


def body(images, captions, caption_owner, caption_count, log_scale, bias):
    D = images.shape[1]
    W = D + EXTRA
    ny = Y_HI * Y_LO
    nxy = NX * ny
    rows = PAIR * nxy
    all_pairs = PAIR * 2 * NX * ny * NZ
    vmem = pl.BlockSpec(memory_space=pltpu.VMEM)
    half = jnp.bfloat16
    loss, gi, gc = pl.pallas_call(
        functools.partial(kernel, all_pairs),
        out_shape=(
            jax.ShapeDtypeStruct((PAIR,), jnp.float32),
            jax.ShapeDtypeStruct((PAIR, D), jnp.float32),
            jax.ShapeDtypeStruct((SLOT, D), jnp.float32),
        ),
        in_specs=[pl.BlockSpec(memory_space=pltpu.HBM)] * 3 + [pl.BlockSpec(memory_space=pltpu.SMEM)] * 3,
        out_specs=(vmem, vmem, vmem),
        scratch_shapes=[
            pltpu.VMEM((PAIR, D), half),
            pltpu.VMEM((SLOT, D), half),
            pltpu.SMEM((SLOT,), jnp.int32),
            pltpu.VMEM((nxy, PAIR, D), half),
            pltpu.VMEM((NZ, SLOT, D), half),
            pltpu.VMEM((2, rows, D), half),
            pltpu.VMEM((NZ * SLOT, D), half),
            pltpu.VMEM((rows, W), half),
            pltpu.VMEM((rows, W), half),
            pltpu.VMEM((nxy, PAIR, W), half),
            pltpu.VMEM((nxy, PAIR, W), half),
            pltpu.VMEM((NZ, SLOT, D), half),
            pltpu.VMEM((NZ, SLOT, D), half),
            pltpu.SemaphoreType.DMA((3,)),
            pltpu.SemaphoreType.DMA((9,)),
            pltpu.SemaphoreType.DMA((9,)),
        ],
        compiler_params=pltpu.CompilerParams(
            collective_id=0, has_side_effects=True, vmem_limit_bytes=32 * 1024 * 1024
        ),
    )(
        *[pltpu.with_memory_space_constraint(a, pltpu.HBM) for a in (images, captions, caption_owner)],
        caption_count, log_scale, bias,
    )
    loss, gi, gc = pl.pallas_call(
        hand_over,
        out_shape=(
            jax.ShapeDtypeStruct((PAIR,), jnp.float32),
            jax.ShapeDtypeStruct((PAIR, D), jnp.float32),
            jax.ShapeDtypeStruct((SLOT, D), jnp.float32),
        ),
        in_specs=[vmem] * 3,
        out_specs=(vmem, vmem, vmem),
    )(loss, gi, gc)
    return loss, gi, gc


def solution(mesh):
    placed = (
        P(("dp", "pack"), None),
        P(("dp", "pack"), None),
        P(("dp", "pack")),
        P(("dp", "pack")),
        P(),
        P(),
    )
    return jax.shard_map(
        body,
        mesh=mesh,
        in_specs=placed,
        out_specs=(P(("dp", "pack")), P(("dp", "pack"), None), P(("dp", "pack"), None)),
        check_vma=False,
    )
```

```python
import functools

import jax
import jax.numpy as jnp
from jax import lax
from jax.experimental import pallas as pl
from jax.experimental.pallas import tpu as pltpu
from jax.sharding import PartitionSpec as P

MESH = pl.DeviceIdType.MESH
EPS = 1e-06
NX, Y_HI, Y_LO, NZ = 4, 2, 4, 12
PAIR, SLOT = 2, 4
EXTRA = 128


def normalize(rows):
    inverse = lax.rsqrt(jnp.sum(rows * rows, axis=-1, keepdims=True) + EPS)
    return rows * inverse, inverse


def unnormalize(unit, inverse, upstream):
    return inverse * (upstream - unit * jnp.sum(unit * upstream, axis=-1, keepdims=True))


def softplus(v):
    return jnp.maximum(v, 0.0) + jnp.log1p(jnp.exp(-jnp.abs(v)))


def split_sum(total):
    high = total.astype(jnp.bfloat16)
    low = (total - high.astype(jnp.float32)).astype(jnp.bfloat16)
    lane = lax.broadcasted_iota(jnp.int32, (total.shape[0], EXTRA), 1)
    return jnp.where(lane == 0, high.astype(jnp.float32), jnp.where(lane == 1, low.astype(jnp.float32), 0.0))


def kernel(
    all_pairs,
    images_hbm, captions_hbm, owner_hbm, count_ref, scale_ref, bias_ref,
    loss_ref, gi_ref, gc_ref,
    images_ref, captions_ref, owner_ref,
    xy_in, z_in, core_out, core_in, xy_out, xy_back, z_out, z_back,
    load, send, recv,
):
    D = images_ref.shape[1]
    ny = Y_HI * Y_LO
    nxy = NX * ny
    rows = PAIR * nxy
    columns = SLOT * NZ
    dp = lax.axis_index("dp")
    pack = lax.axis_index("pack")
    core = lax.rem(dp, 2)
    z = lax.rem(dp // 2, NZ)
    y_lo = dp // (2 * NZ)
    x = pack // Y_HI
    y_hi = lax.rem(pack, Y_HI)
    y = y_hi * Y_LO + y_lo

    def device(xx, yy, zz, cc):
        return ((lax.rem(yy, Y_LO) * NZ + zz) * 2 + cc, xx * Y_HI + yy // Y_LO)

    def at_xy(k, way, cc):
        kx, ky = k % NX, k // NX
        return device(lax.rem(x + way * kx + NX, NX), lax.rem(y + way * ky + ny, ny), z, cc)

    def at_z(k):
        return device(x, y, lax.rem(z + k + NZ, NZ), core)

    def hops(k, n):
        return min(k, n - k)

    other = 1 - core
    sibling = device(x, y, z, other)
    order = sorted(range(nxy), key=lambda k: hops(k % NX, NX) + hops(k // NX, ny))
    last = nxy - 1
    far = order[last]
    near = pl.ds(1, nxy - 2)
    far_z = sorted(range(1, NZ), key=lambda k: -hops(k, NZ))

    loads = [
        pltpu.make_async_copy(src, dst, load.at[i])
        for i, (src, dst) in enumerate((
            (images_hbm, images_ref), (captions_hbm, captions_ref), (owner_hbm, owner_ref),
        ))
    ]
    for one in loads:
        one.start()
    barrier = pltpu.get_barrier_semaphore()
    partners = [at_xy(far, 1, core), at_xy(far, 1, other)]
    partners += [at_z(k) for k in far_z]
    partners += [at_xy(order[p], 1, core) for p in range(last - 1, 0, -1)]
    partners += [sibling]
    for partner in partners:
        pl.semaphore_signal(barrier, inc=1, device_id=partner, device_id_type=MESH)

    loads[0].wait()
    image_unit, image_inv = normalize(images_ref[...].astype(jnp.float32))
    xy_in[0, 0] = image_unit.astype(jnp.bfloat16)
    loads[1].wait()
    slot_row = lax.broadcasted_iota(jnp.int32, (SLOT, 1), 0)
    filled = slot_row < count_ref[0]
    captions = jnp.where(filled, captions_ref[...].astype(jnp.float32), 0.0)
    text_unit, text_inv = normalize(captions)
    z_in[0] = text_unit.astype(jnp.bfloat16)
    loads[2].wait()

    own = lax.broadcasted_iota(jnp.int32, (rows, columns), 0)
    column = lax.broadcasted_iota(jnp.int32, (rows, columns), 1)
    pair = jnp.full_like(own, -1)
    for p, k in enumerate(order):
        kx, ky = k % NX, k // NX
        if ky % Y_LO == 0:
            first = lax.rem(x - kx + NX, NX) * Y_HI + lax.rem(y_hi - ky // Y_LO + Y_HI, Y_HI)
            pair = jnp.where(own // PAIR == p, first * PAIR + lax.rem(own, PAIR), pair)
    owner = jnp.full_like(column, -2)
    for s in range(SLOT):
        owner = jnp.where(jnp.logical_and(column == s, s < count_ref[0]), owner_ref[s], owner)
    sign = jnp.where(pair == owner, -1.0, 1.0)
    scale = jnp.exp(jnp.full((1, 1), scale_ref[0], jnp.float32))
    bias = jnp.full((1, 1), bias_ref[0], jnp.float32)

    pl.semaphore_wait(barrier, len(partners))

    sent = []

    def copy(src, dst, sem, to):
        pltpu.make_async_remote_copy(
            src_ref=src, dst_ref=dst, send_sem=send.at[sem], recv_sem=recv.at[sem],
            device_id=to, device_id_type=MESH,
        ).start()

    def arrived(ref, sem):
        pltpu.make_async_copy(ref, ref, recv.at[sem]).wait()

    copy(xy_in.at[0, 0], xy_in.at[1, last], 9, at_xy(far, 1, other))
    sent.append((xy_in.at[1, last], 9))
    copy(xy_in.at[0, 0], xy_in.at[0, last], 8, at_xy(far, 1, core))
    sent.append((xy_in.at[0, last], 8))
    for k in far_z:
        copy(z_in.at[0], z_in.at[k], 1, at_z(k))
    sent.append((z_in.at[pl.ds(1, NZ - 1)], 1))
    for p in range(last - 1, 0, -1):
        copy(xy_in.at[0, 0], xy_in.at[0, p], 0, at_xy(order[p], 1, core))
    sent.append((xy_in.at[0, near], 0))

    arrived(xy_in.at[0, near], 0)
    copy(xy_in.at[0, pl.ds(0, last)], xy_in.at[1, pl.ds(0, last)], 3, sibling)
    sent.append((xy_in.at[1, pl.ds(0, last)], 3))

    def weigh(image_rows, sign):
        dots = lax.dot_general(image_rows, text_rows, (((1,), (1,)), ((), ())), preferred_element_type=jnp.float32)
        v = sign * (scale * dots + bias)
        small = jnp.exp(-jnp.abs(v))
        losses = jnp.sum(jnp.maximum(v, 0.0) + jnp.log1p(small), axis=1, keepdims=True)
        weights = (sign * jnp.where(v >= 0.0, 1.0, small) / (1.0 + small)).astype(jnp.bfloat16)
        image_grad = scale * jnp.dot(weights, text_rows, preferred_element_type=jnp.float32)
        return losses, weights, image_grad

    def for_texts(weights, image_rows):
        return lax.dot_general(weights, image_rows, (((0,), (0,)), ((), ())), preferred_element_type=jnp.float32)

    def pack_up(p, grad, pieces):
        xy_out[p, :, :D] = grad.astype(jnp.bfloat16)
        xy_out[p, :, D:] = pieces.astype(jnp.bfloat16)

    arrived(z_in.at[pl.ds(1, NZ - 1)], 1)
    text_rows = z_in[...].reshape(columns, D)
    arrived(xy_in.at[0, last], 8)
    mine_rows = xy_in[0].reshape(rows, D)
    loss, weights, mine = weigh(mine_rows, sign)
    pack_up(last, mine[rows - PAIR:], split_sum(loss[rows - PAIR:]))
    copy(xy_out.at[last], xy_back.at[last], 10, at_xy(far, -1, core))
    sent.append((xy_out.at[last], 10))
    text_grad = for_texts(weights, mine_rows)

    arrived(xy_in.at[1, last], 9)
    arrived(xy_in.at[1, pl.ds(0, last)], 3)
    their_rows = xy_in[1].reshape(rows, D)
    losses, weights, theirs = weigh(their_rows, 1.0)
    pieces = split_sum(losses)
    pack_up(nxy, theirs[rows - PAIR:], pieces[rows - PAIR:])
    copy(xy_out.at[nxy], xy_back.at[nxy], 11, at_xy(far, -1, other))
    sent.append((xy_out.at[nxy], 11))
    core_out[:, :D] = theirs.astype(jnp.bfloat16)
    core_out[:, D:] = pieces.astype(jnp.bfloat16)
    copy(core_out, core_in, 5, sibling)
    sent.append((core_out, 5))

    text_grad = scale * (text_grad + for_texts(weights, their_rows))
    for k in far_z:
        z_out[k] = text_grad[k * SLOT:(k + 1) * SLOT].astype(jnp.bfloat16)
        copy(z_out.at[k], z_back.at[k], 6, at_z(-k))
    sent.append((z_out.at[pl.ds(1, NZ - 1)], 6))

    arrived(core_in, 5)
    mine = mine + core_in[:, :D].astype(jnp.float32)
    loss = loss + jnp.sum(core_in[:, D:].astype(jnp.float32), axis=1, keepdims=True)
    pieces = split_sum(loss)
    for p in range(last - 1, 0, -1):
        part = slice(p * PAIR, (p + 1) * PAIR)
        pack_up(p, mine[part], pieces[part])
        copy(xy_out.at[p], xy_back.at[p], 7, at_xy(order[p], -1, core))
    sent.append((xy_out.at[near], 7))

    text_mine = text_grad[:SLOT]
    arrived(z_back.at[pl.ds(1, NZ - 1)], 6)
    for k in range(1, NZ):
        text_mine = text_mine + z_back[k].astype(jnp.float32)
    gc_ref[...] = jnp.where(filled, unnormalize(text_unit, text_inv, text_mine), 0.0)

    arrived(xy_back.at[last], 10)
    arrived(xy_back.at[nxy], 11)
    arrived(xy_back.at[near], 7)
    total = xy_back[1].astype(jnp.float32)
    for p in range(2, nxy + 1):
        total = total + xy_back[p].astype(jnp.float32)
    gi_ref[...] = unnormalize(image_unit, image_inv, mine[:PAIR] + total[:, :D])
    loss = loss[:PAIR] + jnp.sum(total[:, D:], axis=1, keepdims=True)
    loss_ref[...] = (loss / all_pairs - softplus(bias))[:, 0]

    for ref, sem in sent:
        pltpu.make_async_copy(ref, ref, send.at[sem]).wait()


def hand_over(loss_in, gi_in, gc_in, loss_ref, gi_ref, gc_ref):
    loss_ref[...] = loss_in[...]
    gi_ref[...] = gi_in[...]
    gc_ref[...] = gc_in[...]


def body(images, captions, caption_owner, caption_count, log_scale, bias):
    D = images.shape[1]
    W = D + EXTRA
    ny = Y_HI * Y_LO
    nxy = NX * ny
    rows = PAIR * nxy
    all_pairs = PAIR * 2 * NX * ny * NZ
    vmem = pl.BlockSpec(memory_space=pltpu.VMEM)
    half = jnp.bfloat16
    loss, gi, gc = pl.pallas_call(
        functools.partial(kernel, all_pairs),
        out_shape=(
            jax.ShapeDtypeStruct((PAIR,), jnp.float32),
            jax.ShapeDtypeStruct((PAIR, D), jnp.float32),
            jax.ShapeDtypeStruct((SLOT, D), jnp.float32),
        ),
        in_specs=[pl.BlockSpec(memory_space=pltpu.HBM)] * 3 + [pl.BlockSpec(memory_space=pltpu.SMEM)] * 3,
        out_specs=(vmem, vmem, vmem),
        scratch_shapes=[
            pltpu.VMEM((PAIR, D), half),
            pltpu.VMEM((SLOT, D), half),
            pltpu.SMEM((SLOT,), jnp.int32),
            pltpu.VMEM((2, nxy, PAIR, D), half),
            pltpu.VMEM((NZ, SLOT, D), half),
            pltpu.VMEM((rows, W), half),
            pltpu.VMEM((rows, W), half),
            pltpu.VMEM((nxy + 1, PAIR, W), half),
            pltpu.VMEM((nxy + 1, PAIR, W), half),
            pltpu.VMEM((NZ, SLOT, D), half),
            pltpu.VMEM((NZ, SLOT, D), half),
            pltpu.SemaphoreType.DMA((3,)),
            pltpu.SemaphoreType.DMA((12,)),
            pltpu.SemaphoreType.DMA((12,)),
        ],
        compiler_params=pltpu.CompilerParams(
            collective_id=0, has_side_effects=True, vmem_limit_bytes=32 * 1024 * 1024
        ),
    )(
        *[pltpu.with_memory_space_constraint(a, pltpu.HBM) for a in (images, captions, caption_owner)],
        caption_count, log_scale, bias,
    )
    loss, gi, gc = pl.pallas_call(
        hand_over,
        out_shape=(
            jax.ShapeDtypeStruct((PAIR,), jnp.float32),
            jax.ShapeDtypeStruct((PAIR, D), jnp.float32),
            jax.ShapeDtypeStruct((SLOT, D), jnp.float32),
        ),
        in_specs=[vmem] * 3,
        out_specs=(vmem, vmem, vmem),
    )(loss, gi, gc)
    return loss, gi, gc


def solution(mesh):
    placed = (
        P(("dp", "pack"), None),
        P(("dp", "pack"), None),
        P(("dp", "pack")),
        P(("dp", "pack")),
        P(),
        P(),
    )
    return jax.shard_map(
        body,
        mesh=mesh,
        in_specs=placed,
        out_specs=(P(("dp", "pack")), P(("dp", "pack"), None), P(("dp", "pack"), None)),
        check_vma=False,
    )
```

```python
import functools

import jax
import jax.numpy as jnp
from jax import lax
from jax.experimental import pallas as pl
from jax.experimental.pallas import tpu as pltpu
from jax.sharding import PartitionSpec as P

MESH = pl.DeviceIdType.MESH
EPS = 1e-06
NX, Y_HI, Y_LO, NZ = 4, 2, 4, 12
PAIR, SLOT = 2, 4
EXTRA = 128


def normalize(rows):
    inverse = lax.rsqrt(jnp.sum(rows * rows, axis=-1, keepdims=True) + EPS)
    return rows * inverse, inverse


def unnormalize(unit, inverse, upstream):
    return inverse * (upstream - unit * jnp.sum(unit * upstream, axis=-1, keepdims=True))


def softplus(v):
    return jnp.maximum(v, 0.0) + jnp.log1p(jnp.exp(-jnp.abs(v)))


def split_sum(total):
    high = total.astype(jnp.bfloat16)
    low = (total - high.astype(jnp.float32)).astype(jnp.bfloat16)
    lane = lax.broadcasted_iota(jnp.int32, (total.shape[0], EXTRA), 1)
    return jnp.where(lane == 0, high.astype(jnp.float32), jnp.where(lane == 1, low.astype(jnp.float32), 0.0))


def kernel(
    all_pairs,
    images_hbm, captions_hbm, owner_hbm, count_ref, scale_ref, bias_ref,
    loss_ref, gi_ref, gc_ref,
    images_ref, captions_ref, owner_ref,
    xy_in, z_in, x_all, texts,
    core_out, core_in, xy_out, xy_back, z_out, z_back,
    load, send, recv,
):
    D = images_ref.shape[1]
    ny = Y_HI * Y_LO
    nxy = NX * ny
    rows = PAIR * nxy
    loads = [
        pltpu.make_async_copy(src, dst, load.at[i])
        for i, (src, dst) in enumerate((
            (images_hbm, images_ref), (captions_hbm, captions_ref), (owner_hbm, owner_ref),
        ))
    ]
    for one in loads:
        one.start()
    dp = lax.axis_index("dp")
    pack = lax.axis_index("pack")
    core = lax.rem(dp, 2)
    z = lax.rem(dp // 2, NZ)
    y_lo = dp // (2 * NZ)
    x = pack // Y_HI
    y_hi = lax.rem(pack, Y_HI)
    y = y_hi * Y_LO + y_lo

    def device(xx, yy, zz, cc):
        return ((lax.rem(yy, Y_LO) * NZ + zz) * 2 + cc, xx * Y_HI + yy // Y_LO)

    def at_xy(k, way):
        kx, ky = k % NX, k // NX
        return device(lax.rem(x + way * kx + NX, NX), lax.rem(y + way * ky + ny, ny), z, core)

    def at_z(k):
        return device(x, y, lax.rem(z + k + NZ, NZ), core)

    sibling = device(x, y, z, 1 - core)

    def hops(k, n):
        return min(k, n - k)

    far_xy = sorted(range(1, nxy), key=lambda k: -hops(k % NX, NX) - hops(k // NX, ny))
    far_z = sorted(range(1, NZ), key=lambda k: -hops(k, NZ))

    barrier = pltpu.get_barrier_semaphore()
    partners = [sibling]
    partners += [at_z(k) for k in far_z]
    partners += [at_xy(k, 1) for k in far_xy]
    for partner in partners:
        pl.semaphore_signal(barrier, inc=1, device_id=partner, device_id_type=MESH)

    loads[0].wait()
    image_unit, image_inv = normalize(images_ref[...].astype(jnp.float32))
    xy_in[0] = image_unit.astype(jnp.bfloat16)
    loads[1].wait()
    slot_row = lax.broadcasted_iota(jnp.int32, (SLOT, 1), 0)
    filled = slot_row < count_ref[0]
    captions = jnp.where(filled, captions_ref[...].astype(jnp.float32), 0.0)
    text_unit, text_inv = normalize(captions)
    z_in[0] = text_unit.astype(jnp.bfloat16)

    pl.semaphore_wait(barrier, len(partners))

    sent = []

    def copy(src, dst, sem, to):
        pltpu.make_async_remote_copy(
            src_ref=src, dst_ref=dst, send_sem=send.at[sem], recv_sem=recv.at[sem],
            device_id=to, device_id_type=MESH,
        ).start()

    def arrived(ref, sem):
        pltpu.make_async_copy(ref, ref, recv.at[sem]).wait()

    for k in far_z:
        copy(z_in.at[0], z_in.at[k], 1, at_z(k))
    sent.append((z_in.at[pl.ds(1, NZ - 1)], 1))
    for k in far_xy:
        copy(xy_in.at[0], xy_in.at[k], 0, at_xy(k, 1))
    sent.append((xy_in.at[pl.ds(1, nxy - 1)], 0))

    arrived(xy_in.at[pl.ds(1, nxy - 1)], 0)
    x_all[0] = xy_in[...].reshape(rows, D)
    copy(x_all.at[0], x_all.at[1], 3, sibling)
    sent.append((x_all.at[1], 3))

    arrived(z_in.at[pl.ds(1, NZ - 1)], 1)
    texts[...] = z_in[...].reshape(NZ * SLOT, D)

    loads[2].wait()
    own = lax.broadcasted_iota(jnp.int32, (2 * rows, NZ * SLOT), 0)
    column = lax.broadcasted_iota(jnp.int32, (2 * rows, NZ * SLOT), 1)
    slot = lax.rem(own, rows) // PAIR
    y_slot = slot // NX
    from_x = lax.rem(x - lax.rem(slot, NX) + NX, NX)
    from_y_hi = lax.rem(y_hi - y_slot // Y_LO + Y_HI, Y_HI)
    pair = (from_x * Y_HI + from_y_hi) * PAIR + lax.rem(own, PAIR)
    pair = jnp.where(jnp.logical_and(own < rows, lax.rem(y_slot, Y_LO) == 0), pair, -1)
    owner = jnp.full_like(column, -2)
    for s in range(SLOT):
        owner = jnp.where(jnp.logical_and(column == s, s < count_ref[0]), owner_ref[s], owner)
    sign = jnp.where(pair == owner, -1.0, 1.0)

    scale = jnp.exp(jnp.full((1, 1), scale_ref[0], jnp.float32))
    bias = jnp.full((1, 1), bias_ref[0], jnp.float32)

    arrived(x_all.at[1], 3)

    image_rows = x_all[...].reshape(2 * rows, D)
    text_rows = texts[...]
    dots = lax.dot_general(image_rows, text_rows, (((1,), (1,)), ((), ())), preferred_element_type=jnp.float32)
    v = sign * (scale * dots + bias)
    small = jnp.exp(-jnp.abs(v))
    losses = jnp.sum(jnp.maximum(v, 0.0) + jnp.log1p(small), axis=1, keepdims=True)
    weights = (sign * jnp.where(v >= 0.0, 1.0, small) / (1.0 + small)).astype(jnp.bfloat16)

    core_out[:, :D] = (scale * jnp.dot(weights[rows:], text_rows, preferred_element_type=jnp.float32)).astype(jnp.bfloat16)
    core_out[:, D:] = split_sum(losses[rows:]).astype(jnp.bfloat16)
    copy(core_out, core_in, 5, sibling)
    sent.append((core_out, 5))

    text_grad = scale * lax.dot_general(weights, image_rows, (((0,), (0,)), ((), ())), preferred_element_type=jnp.float32)
    for k in far_z:
        z_out[k] = text_grad[k * SLOT:(k + 1) * SLOT].astype(jnp.bfloat16)
        copy(z_out.at[k], z_back.at[k], 6, at_z(-k))
    sent.append((z_out.at[pl.ds(1, NZ - 1)], 6))

    mine = scale * jnp.dot(weights[:rows], text_rows, preferred_element_type=jnp.float32)
    arrived(core_in, 5)
    mine = mine + core_in[:, :D].astype(jnp.float32)
    other = core_in[:, D:].astype(jnp.float32)
    loss = losses[:rows] + jnp.sum(other, axis=1, keepdims=True)
    pieces = split_sum(loss)
    for k in far_xy:
        part = slice(k * PAIR, (k + 1) * PAIR)
        xy_out[k, :, :D] = mine[part].astype(jnp.bfloat16)
        xy_out[k, :, D:] = pieces[part].astype(jnp.bfloat16)
        copy(xy_out.at[k], xy_back.at[k], 7, at_xy(k, -1))
    sent.append((xy_out.at[pl.ds(1, nxy - 1)], 7))
    mine, loss = mine[:PAIR], loss[:PAIR]

    text_mine = text_grad[:SLOT]
    arrived(z_back.at[pl.ds(1, NZ - 1)], 6)
    for k in range(1, NZ):
        text_mine = text_mine + z_back[k].astype(jnp.float32)
    gc_ref[...] = jnp.where(filled, unnormalize(text_unit, text_inv, text_mine), 0.0)

    arrived(xy_back.at[pl.ds(1, nxy - 1)], 7)
    for k in range(1, nxy):
        mine = mine + xy_back[k, :, :D].astype(jnp.float32)
        loss = loss + jnp.sum(xy_back[k, :, D:].astype(jnp.float32), axis=1, keepdims=True)
    gi_ref[...] = unnormalize(image_unit, image_inv, mine)
    loss_ref[...] = (loss / all_pairs - softplus(bias))[:, 0]

    for ref, sem in sent:
        pltpu.make_async_copy(ref, ref, send.at[sem]).wait()


def hand_over(loss_in, gi_in, gc_in, loss_ref, gi_ref, gc_ref):
    loss_ref[...] = loss_in[...]
    gi_ref[...] = gi_in[...]
    gc_ref[...] = gc_in[...]


def body(images, captions, caption_owner, caption_count, log_scale, bias):
    D = images.shape[1]
    W = D + EXTRA
    ny = Y_HI * Y_LO
    nxy = NX * ny
    rows = PAIR * nxy
    all_pairs = PAIR * 2 * NX * ny * NZ
    vmem = pl.BlockSpec(memory_space=pltpu.VMEM)
    half = jnp.bfloat16
    loss, gi, gc = pl.pallas_call(
        functools.partial(kernel, all_pairs),
        out_shape=(
            jax.ShapeDtypeStruct((PAIR,), jnp.float32),
            jax.ShapeDtypeStruct((PAIR, D), jnp.float32),
            jax.ShapeDtypeStruct((SLOT, D), jnp.float32),
        ),
        in_specs=[pl.BlockSpec(memory_space=pltpu.HBM)] * 3 + [pl.BlockSpec(memory_space=pltpu.SMEM)] * 3,
        out_specs=(vmem, vmem, vmem),
        scratch_shapes=[
            pltpu.VMEM((PAIR, D), half),
            pltpu.VMEM((SLOT, D), half),
            pltpu.SMEM((SLOT,), jnp.int32),
            pltpu.VMEM((nxy, PAIR, D), half),
            pltpu.VMEM((NZ, SLOT, D), half),
            pltpu.VMEM((2, rows, D), half),
            pltpu.VMEM((NZ * SLOT, D), half),
            pltpu.VMEM((rows, W), half),
            pltpu.VMEM((rows, W), half),
            pltpu.VMEM((nxy, PAIR, W), half),
            pltpu.VMEM((nxy, PAIR, W), half),
            pltpu.VMEM((NZ, SLOT, D), half),
            pltpu.VMEM((NZ, SLOT, D), half),
            pltpu.SemaphoreType.DMA((3,)),
            pltpu.SemaphoreType.DMA((9,)),
            pltpu.SemaphoreType.DMA((9,)),
        ],
        compiler_params=pltpu.CompilerParams(
            collective_id=0, has_side_effects=True, vmem_limit_bytes=8 * 1024 * 1024
        ),
    )(
        *[pltpu.with_memory_space_constraint(a, pltpu.HBM) for a in (images, captions, caption_owner)],
        caption_count, log_scale, bias,
    )
    loss, gi, gc = pl.pallas_call(
        hand_over,
        out_shape=(
            jax.ShapeDtypeStruct((PAIR,), jnp.float32),
            jax.ShapeDtypeStruct((PAIR, D), jnp.float32),
            jax.ShapeDtypeStruct((SLOT, D), jnp.float32),
        ),
        in_specs=[vmem] * 3,
        out_specs=(vmem, vmem, vmem),
    )(loss, gi, gc)
    return loss, gi, gc


def solution(mesh):
    placed = (
        P(("dp", "pack"), None),
        P(("dp", "pack"), None),
        P(("dp", "pack")),
        P(("dp", "pack")),
        P(),
        P(),
    )
    return jax.shard_map(
        body,
        mesh=mesh,
        in_specs=placed,
        out_specs=(P(("dp", "pack")), P(("dp", "pack"), None), P(("dp", "pack"), None)),
        check_vma=False,
    )
```

```python
import functools

import jax
import jax.numpy as jnp
from jax import lax
from jax.experimental import pallas as pl
from jax.experimental.pallas import tpu as pltpu
from jax.sharding import PartitionSpec as P

MESH = pl.DeviceIdType.MESH
EPS = 1e-06
NX, Y_HI, Y_LO, NZ = 4, 2, 4, 12
PAIR, SLOT = 2, 4
EXTRA = 128


def normalize(rows):
    inverse = lax.rsqrt(jnp.sum(rows * rows, axis=-1, keepdims=True) + EPS)
    return rows * inverse, inverse


def unnormalize(unit, inverse, upstream):
    return inverse * (upstream - unit * jnp.sum(unit * upstream, axis=-1, keepdims=True))


def softplus(v):
    return jnp.maximum(v, 0.0) + jnp.log1p(jnp.exp(-jnp.abs(v)))


def split_sum(total):
    high = total.astype(jnp.bfloat16)
    low = (total - high.astype(jnp.float32)).astype(jnp.bfloat16)
    lane = lax.broadcasted_iota(jnp.int32, (total.shape[0], EXTRA), 1)
    return jnp.where(lane == 0, high.astype(jnp.float32), jnp.where(lane == 1, low.astype(jnp.float32), 0.0))


def kernel(
    all_pairs,
    images_hbm, captions_hbm, owner_hbm, count_ref, scale_ref, bias_ref,
    loss_ref, gi_ref, gc_ref,
    images_ref, captions_ref, owner_ref,
    image_mine, text_mine, mine_info, their_info,
    xy_in, z_in, image_rows, text_rows, xy_out, xy_back, z_out, z_back,
    load, send, recv, ready,
):
    D = images_ref.shape[1]
    ny = Y_HI * Y_LO
    nxy = NX * ny
    rows = PAIR * nxy
    columns = SLOT * NZ
    dp = lax.axis_index("dp")
    pack = lax.axis_index("pack")
    core = lax.rem(dp, 2)
    z = lax.rem(dp // 2, NZ)
    y_lo = dp // (2 * NZ)
    x = pack // Y_HI
    y_hi = lax.rem(pack, Y_HI)
    y = y_hi * Y_LO + y_lo

    def device(xx, yy, zz, cc):
        return ((lax.rem(yy, Y_LO) * NZ + zz) * 2 + cc, xx * Y_HI + yy // Y_LO)

    def at_xy(k, way, cc):
        kx, ky = k % NX, k // NX
        return device(lax.rem(x + way * kx + NX, NX), lax.rem(y + way * ky + ny, ny), z, cc)

    def at_z(k, way, cc):
        return device(x, y, lax.rem(z + way * k + NZ, NZ), cc)

    sibling = device(x, y, z, 1 - core)

    def hops(k, n):
        return min(k, n - k)

    far_xy = sorted(range(1, nxy), key=lambda k: -hops(k % NX, NX) - hops(k // NX, ny))
    far_z = sorted(range(1, NZ), key=lambda k: -hops(k, NZ))

    barrier = pltpu.get_barrier_semaphore()

    def greet(partner):
        pl.semaphore_signal(barrier, inc=1, device_id=partner, device_id_type=MESH)

    greet(sibling)

    @pl.when(core == 0)
    def _():
        for k in far_z:
            greet(at_z(k, 1, 0))

    @pl.when(core == 1)
    def _():
        for k in far_xy:
            greet(at_xy(k, 1, 1))

    loads = [
        pltpu.make_async_copy(src, dst, load.at[i])
        for i, (src, dst) in enumerate((
            (images_hbm, images_ref), (captions_hbm, captions_ref), (owner_hbm, owner_ref),
        ))
    ]
    for one in loads:
        one.start()
    loads[0].wait()
    image_unit, image_inv = normalize(images_ref[...].astype(jnp.float32))
    image_mine[0] = image_unit.astype(jnp.bfloat16)
    loads[1].wait()
    slot_row = lax.broadcasted_iota(jnp.int32, (SLOT, 1), 0)
    filled = slot_row < count_ref[0]
    captions = jnp.where(filled, captions_ref[...].astype(jnp.float32), 0.0)
    text_unit, text_inv = normalize(captions)
    text_mine[0] = text_unit.astype(jnp.bfloat16)
    loads[2].wait()
    lane = lax.broadcasted_iota(jnp.int32, mine_info.shape, 1)
    info = jnp.full(mine_info.shape, -2, jnp.int32)
    for s in range(SLOT):
        info = jnp.where(jnp.logical_and(lane == core * columns + s, s < count_ref[0]), owner_ref[s], info)
    mine_info[...] = info

    def copy(src, dst, sem, to):
        pltpu.make_async_remote_copy(
            src_ref=src, dst_ref=dst, send_sem=send.at[sem], recv_sem=recv.at[sem],
            device_id=to, device_id_type=MESH,
        ).start()

    def arrived(ref, sem):
        pltpu.make_async_copy(ref, ref, recv.at[sem]).wait()

    def left(ref, sem):
        pltpu.make_async_copy(ref, ref, send.at[sem]).wait()

    def announce():
        pl.semaphore_signal(ready.at[0], inc=1, device_id=sibling, device_id_type=MESH)

    def send_images(slot):
        for k in far_xy:
            copy(image_mine.at[0], xy_in.at[slot + k], 0, at_xy(k, 1, 1))

    def send_texts(slot):
        for k in far_z:
            copy(text_mine.at[0], z_in.at[slot + k], 1, at_z(k, 1, 0))

    @pl.when(core == 0)
    def _():
        pl.semaphore_wait(barrier, NZ)
        announce()
        send_texts(0)
        copy(mine_info, their_info, 2, sibling)
        copy(image_mine.at[0], xy_in.at[nxy], 0, sibling)
        z_in[0] = text_mine[0]
        pl.semaphore_wait(ready.at[0], 1)
        send_images(nxy)
        arrived(z_in.at[pl.ds(1, 2 * NZ - 1)], 1)
        text_rows[...] = z_in[...].reshape(2 * columns, D)
        copy(text_rows, text_rows, 4, sibling)

    @pl.when(core == 1)
    def _():
        pl.semaphore_wait(barrier, nxy)
        announce()
        send_images(0)
        copy(mine_info, their_info, 2, sibling)
        copy(text_mine.at[0], z_in.at[NZ], 1, sibling)
        xy_in[0] = image_mine[0]
        pl.semaphore_wait(ready.at[0], 1)
        send_texts(NZ)
        arrived(xy_in.at[pl.ds(1, 2 * nxy - 1)], 0)
        image_rows[...] = xy_in[...].reshape(2 * rows, D)
        copy(image_rows, image_rows, 3, sibling)

    own = lax.broadcasted_iota(jnp.int32, (2 * rows, 2 * columns), 0)
    column = lax.broadcasted_iota(jnp.int32, (2 * rows, 2 * columns), 1)
    slot = lax.rem(own, rows) // PAIR
    y_slot = slot // NX
    from_x = lax.rem(x - lax.rem(slot, NX) + NX, NX)
    from_y_hi = lax.rem(y_hi - y_slot // Y_LO + Y_HI, Y_HI)
    pair = (from_x * Y_HI + from_y_hi) * PAIR + lax.rem(own, PAIR)
    same = jnp.logical_and(1 - own // rows == column // columns, lax.rem(y_slot, Y_LO) == 0)
    pair = jnp.where(same, pair, -1)
    scale = jnp.exp(jnp.full((1, 1), scale_ref[0], jnp.float32))
    bias = jnp.full((1, 1), bias_ref[0], jnp.float32)
    arrived(their_info, 2)
    owner = jnp.maximum(mine_info[...], their_info[...])[:1, :2 * columns]
    sign = jnp.where(pair == owner, -1.0, 1.0)

    @pl.when(core == 0)
    def _():
        arrived(image_rows, 3)

    @pl.when(core == 1)
    def _():
        arrived(text_rows, 4)

    dots = lax.dot_general(
        image_rows[...], text_rows[...], (((1,), (1,)), ((), ())), preferred_element_type=jnp.float32
    )
    v = sign * (scale * dots + bias)
    small = jnp.exp(-jnp.abs(v))
    weights = (sign * jnp.where(v >= 0.0, 1.0, small) / (1.0 + small)).astype(jnp.bfloat16)

    @pl.when(core == 0)
    def _():
        grad = scale * lax.dot_general(
            weights, image_rows[...], (((0,), (0,)), ((), ())), preferred_element_type=jnp.float32
        )
        z_out[...] = grad.astype(jnp.bfloat16).reshape(2 * NZ, SLOT, D)
        for k in far_z:
            copy(z_out.at[k], z_back.at[k], 5, at_z(k, -1, 0))
            copy(z_out.at[NZ + k], z_back.at[k], 5, at_z(k, -1, 1))
        copy(z_out.at[NZ], z_back.at[0], 5, sibling)
        z_back[0] = z_out[0]
        arrived(z_back.at[pl.ds(1, NZ - 1)], 5)

    @pl.when(core == 1)
    def _():
        losses = jnp.sum(jnp.maximum(v, 0.0) + jnp.log1p(small), axis=1, keepdims=True)
        grad = scale * jnp.dot(weights, text_rows[...], preferred_element_type=jnp.float32)
        xy_out[:, :, :D] = grad.astype(jnp.bfloat16).reshape(2 * nxy, PAIR, D)
        xy_out[:, :, D:] = split_sum(losses).astype(jnp.bfloat16).reshape(2 * nxy, PAIR, EXTRA)
        for k in far_xy:
            copy(xy_out.at[k], xy_back.at[k], 6, at_xy(k, -1, 1))
            copy(xy_out.at[nxy + k], xy_back.at[k], 6, at_xy(k, -1, 0))
        copy(xy_out.at[nxy], xy_back.at[0], 6, sibling)
        xy_back[0] = xy_out[0]
        arrived(z_back, 5)

    text_grad = z_back[0].astype(jnp.float32)
    for k in range(1, NZ):
        text_grad = text_grad + z_back[k].astype(jnp.float32)
    gc_ref[...] = jnp.where(filled, unnormalize(text_unit, text_inv, text_grad), 0.0)

    @pl.when(core == 0)
    def _():
        arrived(xy_back, 6)

    @pl.when(core == 1)
    def _():
        arrived(xy_back.at[pl.ds(1, nxy - 1)], 6)

    total = xy_back[0].astype(jnp.float32)
    for k in range(1, nxy):
        total = total + xy_back[k].astype(jnp.float32)
    gi_ref[...] = unnormalize(image_unit, image_inv, total[:, :D])
    loss = jnp.sum(total[:, D:], axis=1, keepdims=True)
    loss_ref[...] = (loss / all_pairs - softplus(bias))[:, 0]

    left(mine_info, 2)

    @pl.when(core == 0)
    def _():
        left(xy_in.at[pl.ds(0, nxy)], 0)
        left(z_in.at[pl.ds(0, NZ - 1)], 1)
        left(text_rows, 4)
        left(z_out.at[pl.ds(0, 2 * NZ - 1)], 5)

    @pl.when(core == 1)
    def _():
        left(xy_in.at[pl.ds(0, nxy - 1)], 0)
        left(z_in.at[pl.ds(0, NZ)], 1)
        left(image_rows, 3)
        left(xy_out.at[pl.ds(0, 2 * nxy - 1)], 6)


def hand_over(loss_in, gi_in, gc_in, loss_ref, gi_ref, gc_ref):
    loss_ref[...] = loss_in[...]
    gi_ref[...] = gi_in[...]
    gc_ref[...] = gc_in[...]


def body(images, captions, caption_owner, caption_count, log_scale, bias):
    D = images.shape[1]
    W = D + EXTRA
    ny = Y_HI * Y_LO
    nxy = NX * ny
    rows = PAIR * nxy
    all_pairs = PAIR * 2 * NX * ny * NZ
    vmem = pl.BlockSpec(memory_space=pltpu.VMEM)
    half = jnp.bfloat16
    loss, gi, gc = pl.pallas_call(
        functools.partial(kernel, all_pairs),
        out_shape=(
            jax.ShapeDtypeStruct((PAIR,), jnp.float32),
            jax.ShapeDtypeStruct((PAIR, D), jnp.float32),
            jax.ShapeDtypeStruct((SLOT, D), jnp.float32),
        ),
        in_specs=[pl.BlockSpec(memory_space=pltpu.HBM)] * 3 + [pl.BlockSpec(memory_space=pltpu.SMEM)] * 3,
        out_specs=(vmem, vmem, vmem),
        scratch_shapes=[
            pltpu.VMEM((PAIR, D), half),
            pltpu.VMEM((SLOT, D), half),
            pltpu.SMEM((SLOT,), jnp.int32),
            pltpu.VMEM((1, PAIR, D), half),
            pltpu.VMEM((1, SLOT, D), half),
            pltpu.VMEM((8, 128), jnp.int32),
            pltpu.VMEM((8, 128), jnp.int32),
            pltpu.VMEM((2 * nxy, PAIR, D), half),
            pltpu.VMEM((2 * NZ, SLOT, D), half),
            pltpu.VMEM((2 * rows, D), half),
            pltpu.VMEM((2 * NZ * SLOT, D), half),
            pltpu.VMEM((2 * nxy, PAIR, W), half),
            pltpu.VMEM((nxy, PAIR, W), half),
            pltpu.VMEM((2 * NZ, SLOT, D), half),
            pltpu.VMEM((NZ, SLOT, D), half),
            pltpu.SemaphoreType.DMA((3,)),
            pltpu.SemaphoreType.DMA((7,)),
            pltpu.SemaphoreType.DMA((7,)),
            pltpu.SemaphoreType.REGULAR((1,)),
        ],
        compiler_params=pltpu.CompilerParams(
            collective_id=0, has_side_effects=True, vmem_limit_bytes=32 * 1024 * 1024
        ),
    )(
        *[pltpu.with_memory_space_constraint(a, pltpu.HBM) for a in (images, captions, caption_owner)],
        caption_count, log_scale, bias,
    )
    loss, gi, gc = pl.pallas_call(
        hand_over,
        out_shape=(
            jax.ShapeDtypeStruct((PAIR,), jnp.float32),
            jax.ShapeDtypeStruct((PAIR, D), jnp.float32),
            jax.ShapeDtypeStruct((SLOT, D), jnp.float32),
        ),
        in_specs=[vmem] * 3,
        out_specs=(vmem, vmem, vmem),
    )(loss, gi, gc)
    return loss, gi, gc


def solution(mesh):
    placed = (
        P(("dp", "pack"), None),
        P(("dp", "pack"), None),
        P(("dp", "pack")),
        P(("dp", "pack")),
        P(),
        P(),
    )
    return jax.shard_map(
        body,
        mesh=mesh,
        in_specs=placed,
        out_specs=(P(("dp", "pack")), P(("dp", "pack"), None), P(("dp", "pack"), None)),
        check_vma=False,
    )
```
